32 devices in a mesh: rows: 16 (over z, x, core), samp: 2 (over y).
Axes of the slice: x: 2, y: 2, z: 4, core: 2. Of those that a mesh axis runs over, the one named last changes fastest.
Arguments:
- sketch: float32 [256, 49152], P('samp', 'rows'), may hold values from -6 to 6
- probes: float32 [256, 49152], P('samp', 'rows'), may hold values from -6 to 6
- test_leaf: float32 [64, 256], replicated, may hold values from -0.375 to 0.375
- test_parent: float32 [64, 256], replicated, may hold values from -0.375 to 0.375
- leaf_far: int32 [192, 8], P(('rows', 'samp')), may hold values from 0 to 191, as said below
- leaf_count: int32 [192], P(('rows', 'samp')), may hold values from 1 to 8
- parent_far: int32 [96, 8], P(('rows', 'samp')), may hold values from 0 to 95, as said below
- parent_count: int32 [96], P(('rows', 'samp')), may hold values from 1 to 8
Outputs:
- leaf_basis: float32 [64, 49152], P(None, ('rows', 'samp'))
- leaf_coupling: float32 [192, 8, 4096], P(('rows', 'samp'))
- transfer: float32 [96, 64, 128], P(('rows', 'samp'))
- parent_coupling: float32 [96, 8, 4096], P(('rows', 'samp'))
The draws below stay inside these ranges and needn't reach their ends.
Inputs may be any that keep to these rules, and one draw needn't show every extreme that they name: leaf_far[i, k] = j satisfies 2 <= |i - j| <= 6. `parent_far`: with b(p) = p // 3, a partner q of p has b(q) - b(p) a nonzero multiple of 2, at most 4 * 2 in magnitude.
All inputs are finite; a program needn't handle non-finite values.
Results may differ from the reference program's by a relative error of at most 0.0041.
Values may be sent and summed in bfloat16 or wider, within the bound.
A program may use at most 64 MiB of HBM per device.

```python
import jax
import jax.numpy as jnp
from jax import lax

LEAF = 256
RANK = 64
SAMPLES = 256
NFAR = 8
REACH = 4
LEAF_DEV = 6
LEAVES = 192
PARENTS = 96
ORDER = 49152
N_ROWS = 16
N_SAMP = 2


def draw_leaf_far(key, part):
    first_key, second_key = jax.random.split(jax.random.fold_in(key, 11))
    leaf_ids = jnp.arange(LEAVES, dtype=jnp.int32)[:, None]
    distance = 2 + jax.random.randint(first_key, (LEAVES, NFAR), 0, LEAF_DEV - 1)
    direction = jax.random.randint(second_key, (LEAVES, NFAR), 0, 2) * 2 - 1
    partner = leaf_ids + direction * distance
    outside = (partner < 0) | (partner >= LEAVES)
    partner = jnp.where(outside, leaf_ids - direction * distance, partner)
    return partner.astype(jnp.int32)


def draw_leaf_count(key, part):
    return jax.random.randint(jax.random.fold_in(key, 23), (LEAVES,), 1, NFAR + 1).astype(jnp.int32)


def draw_parent_far(key, part):
    first_key, second_key, third_key = jax.random.split(jax.random.fold_in(key, 37), 3)
    per_device = LEAF_DEV // 2
    parent_ids = jnp.arange(PARENTS, dtype=jnp.int32)[:, None]
    block_ids = parent_ids // per_device
    row_ids = block_ids // N_SAMP
    column_ids = block_ids % N_SAMP
    distance = 1 + jax.random.randint(first_key, (PARENTS, NFAR), 0, REACH)
    direction = jax.random.randint(second_key, (PARENTS, NFAR), 0, 2) * 2 - 1
    target_row = row_ids + direction * distance
    outside = (target_row < 0) | (target_row >= N_ROWS)
    target_row = jnp.where(outside, row_ids - direction * distance, target_row)
    within = jax.random.randint(third_key, (PARENTS, NFAR), 0, per_device)
    partner = (target_row * N_SAMP + column_ids) * per_device + within
    return partner.astype(jnp.int32)


def draw_parent_count(key, part):
    return jax.random.randint(jax.random.fold_in(key, 41), (PARENTS,), 1, NFAR + 1).astype(jnp.int32)


def shard_levels(own_key, extent, shards, least, top_value):
    def one(dim, shards_of):
        draws = jax.random.uniform(jax.random.fold_in(jax.random.fold_in(own_key, 6), dim), (shards_of,), jnp.float32, least / len(shards), top_value / len(shards))
        return jnp.repeat(jnp.exp(draws), extent[dim] // shards_of).reshape((-1,) + (1,) * (len(extent) - dim - 1))

    level = one(*shards[0])
    for cut in shards[1:]:
        level = level * one(*cut)
    return level


def gaussian(own_key, shape, width, bound, cuts=(), kind=jnp.bfloat16):
    result = jax.random.normal(own_key, shape, jnp.float32) * width
    if len(cuts) > 0:
        result = shard_levels(own_key, shape, cuts, -0.22, 0.18) * result
    return jnp.clip(result, min=-bound, max=bound).astype(kind)


def setup_inputs(seed: int = 0) -> dict:
    splits = jax.random.split(jax.random.key(seed), 9)
    return {
        "sketch": gaussian(splits[0], (SAMPLES, ORDER), 1.0, 6.0, ((0, 2), (1, 16)), jnp.float32),
        "probes": gaussian(splits[1], (SAMPLES, ORDER), 1.0, 6.0, ((0, 2), (1, 16)), jnp.float32),
        "test_leaf": gaussian(splits[2], (RANK, SAMPLES), SAMPLES ** -0.5, 0.375, (), jnp.float32),
        "test_parent": gaussian(splits[3], (RANK, SAMPLES), SAMPLES ** -0.5, 0.375, (), jnp.float32),
        "leaf_far": draw_leaf_far(jax.random.fold_in(splits[8], 71), 0),
        "leaf_count": draw_leaf_count(jax.random.fold_in(splits[8], 71), 0),
        "parent_far": draw_parent_far(jax.random.fold_in(splits[8], 71), 0),
        "parent_count": draw_parent_count(jax.random.fold_in(splits[8], 71), 0),
    }


highest = lax.Precision.HIGHEST

def orthonormal(blocks):
    gram_matrix = jnp.einsum('nrl,ntl->nrt', blocks, blocks, precision=highest)
    factor = jnp.linalg.cholesky(gram_matrix)
    return jax.scipy.linalg.solve_triangular(factor, blocks, lower=True)

def reference(sketch, probes, test_leaf, test_parent, leaf_far, leaf_count, parent_far, parent_count):
    sketch_cols = sketch.reshape(SAMPLES, LEAVES, LEAF)
    probe_cols = probes.reshape(SAMPLES, LEAVES, LEAF)
    blocks = jnp.einsum('rs,sil->irl', test_leaf, sketch_cols, precision=highest)
    orthobasis = orthonormal(blocks)
    leaf_basis = orthobasis.transpose(1, 0, 2).reshape(RANK, ORDER)
    wproj = jnp.einsum('irl,sil->sir', orthobasis, sketch_cols, precision=highest)
    vproj = jnp.einsum('irl,sil->sir', orthobasis, probe_cols, precision=highest)
    slot_ids = jnp.arange(NFAR, dtype=jnp.int32)
    leaf_mask = (slot_ids[None, :] < leaf_count[:, None]).astype(jnp.float32)
    leaf_terms = []
    for position in range(NFAR):
        partner = vproj[:, leaf_far[:, position], :]
        leaf_terms.append(jnp.einsum('sir,sit->irt', wproj, partner, precision=highest))
    leaf_coupling = jnp.stack(leaf_terms, axis=1) * leaf_mask[:, :, None, None] / SAMPLES
    leaf_coupling = leaf_coupling.reshape(LEAVES, NFAR, RANK * RANK)
    stacked = wproj.reshape(SAMPLES, PARENTS, 2 * RANK)
    vstacked = vproj.reshape(SAMPLES, PARENTS, 2 * RANK)
    parent_blocks = jnp.einsum('rs,spc->prc', test_parent, stacked, precision=highest)
    transfer = orthonormal(parent_blocks)
    wcoarse = jnp.einsum('prc,spc->spr', transfer, stacked, precision=highest).astype(jnp.bfloat16)
    vcoarse = jnp.einsum('prc,spc->spr', transfer, vstacked, precision=highest).astype(jnp.bfloat16)
    parent_mask = (slot_ids[None, :] < parent_count[:, None]).astype(jnp.float32)
    parent_terms = []
    for position in range(NFAR):
        partner = vcoarse[:, parent_far[:, position], :].astype(jnp.float32)
        parent_terms.append(jnp.einsum('spr,spt->prt', wcoarse.astype(jnp.float32), partner, precision=highest))
    parent_coupling = jnp.stack(parent_terms, axis=1) * parent_mask[:, :, None, None] / SAMPLES
    parent_coupling = parent_coupling.reshape(PARENTS, NFAR, RANK * RANK)
    return (leaf_basis, leaf_coupling, transfer, parent_coupling)
```

```python
import functools

import jax
import jax.numpy as jnp
from jax import lax
from jax.experimental import pallas as pl
from jax.experimental.pallas import tpu as pltpu
from jax.sharding import PartitionSpec as P

LEAF = 256
REACH = 4
LANES = 128

F32 = jnp.float32
BF16 = jnp.bfloat16
MESH = pl.DeviceIdType.MESH
highest = lax.Precision.HIGHEST


def dot_nn(a, b, precision=None):
    return lax.dot_general(
        a, b, (((1,), (0,)), ((), ())), precision=precision, preferred_element_type=F32
    )


def dot_nt(a, b, precision=None):
    return lax.dot_general(
        a, b, (((1,), (1,)), ((), ())), precision=precision, preferred_element_type=F32
    )


def split(x):
    hi = x.astype(BF16)
    return hi, (x - hi.astype(F32)).astype(BF16)


def three_pass(dot, a, b):
    a_hi, a_lo = split(a)
    b_hi, b_lo = split(b)
    return dot(a_hi, b_hi) + (dot(a_lo, b_hi) + dot(a_hi, b_lo))


def row_of(x, s):
    return jnp.broadcast_to(x[s : s + 1, :], x.shape)


def inverse_factors(grams):
    rank = grams[0].shape[0]
    lane = lax.broadcasted_iota(jnp.int32, (8, LANES), 1)
    row = lax.broadcasted_iota(jnp.int32, (8, LANES), 0)
    within = lax.rem(lane, rank)
    base = lane - within
    blocks = rank // 8
    results = []
    pairs = [(grams[i], grams[min(i + 1, len(grams) - 1)]) for i in range(0, len(grams), 2)]
    states = []
    for left, right in pairs:
        whole = jnp.concatenate([left, right], axis=1)
        states.append([whole[8 * t : 8 * t + 8, :] for t in range(blocks)])
    scales = [[None] * blocks for _ in pairs]
    for b in range(blocks):
        in_block = (within >= 8 * b) & (within < 8 * b + 8)
        for at, tiles in enumerate(states):
            tile = tiles[b]
            cols = [
                jnp.take_along_axis(tile, base + (8 * b + j), axis=1, mode="promise_in_bounds")
                for j in range(8)
            ]
            scale = jnp.zeros((8, LANES), F32)
            inv_pivots, heads, pivot_rows = [], [], []
            for s in range(8):
                pivot = row_of(cols[s], s)
                inv_pivot = 1.0 / pivot
                scale = jnp.where(row == s, lax.rsqrt(pivot), scale)
                f = jnp.where(row > s, cols[s] * inv_pivot, 0.0)
                head = [None] * 8
                for j in range(s + 1, 8):
                    head[j] = row_of(cols[j], s)
                    cols[j] = cols[j] - f * head[j]
                here = within == 8 * b + s
                pivot_row = jnp.where(here, 1.0, row_of(tile, s))
                tile = jnp.where(here & (row > s), 0.0, tile) - f * pivot_row
                inv_pivots.append(inv_pivot)
                heads.append(head)
                pivot_rows.append(pivot_row)
            scales[at][b] = scale
            tiles[b] = tile
            for t in range(b + 1, blocks):
                tile = tiles[t]
                cols = [
                    jnp.take_along_axis(tile, base + (8 * b + j), axis=1, mode="promise_in_bounds")
                    for j in range(8)
                ]
                for s in range(8):
                    f = cols[s] * inv_pivots[s]
                    for j in range(s + 1, 8):
                        cols[j] = cols[j] - f * heads[s][j]
                    here = within == 8 * b + s
                    tile = jnp.where(here, 0.0, tile) - f * pivot_rows[s]
                tiles[t] = tile
    for at, tiles in enumerate(states):
        done = []
        for b in range(blocks):
            lower = jnp.where(within < row + 8 * b, tiles[b], 0.0)
            lower = jnp.where(within == row + 8 * b, 1.0, lower)
            done.append(lower * scales[at][b])
        whole = jnp.concatenate(done, axis=0)
        results += [whole[:, :rank], whole[:, rank : 2 * rank]]
    return results[: len(grams)]


def put_columns(ref, first, value):
    for c in range(value.shape[1] // LANES):
        ref[c, first : first + value.shape[0], :] = value[:, c * LANES : (c + 1) * LANES]


def even_then_odd(ref, first, rows):
    parts = [
        jnp.concatenate(
            [ref[c, pl.ds(first + o, rows // 2, stride=2), :] for o in (0, 1)], axis=0
        )
        for c in range(ref.shape[0])
    ]
    return jnp.concatenate(parts, axis=1)


def flatten_rows(ref, product, slot, slots):
    half = product.shape[0] // 2
    packed = jnp.concatenate([product[:half], product[half:]], axis=1)
    ref[pl.ds(slot, half, stride=slots), :] = packed


def kernel(
    sizes,
    leaf_far, leaf_count, parent_far, parent_count, test_leaf, test_parent, sketch, probes,
    basis_out, coupling_out, transfer_out, parent_out,
    raw, y_send, o_send, y_hi, y_lo, o_hi, o_lo, w_buf, w_cols, v_all, v_own, a_cols, b_all, flat,
    load_sem, y_sems, o_sems, v_sems, b_sems,
):
    n_rows, n_samp = sizes
    owned, slots = leaf_far.shape
    per_device = parent_far.shape[0]
    rank, samples = test_leaf.shape
    local = samples // n_samp
    width = owned * LEAF
    row, samp = lax.axis_index("rows"), lax.axis_index("samp")
    me = row * n_samp + samp
    last = n_rows * n_samp - 1
    shifts = [s for s in range(-REACH, REACH + 1) if s != 0]

    def at(linear):
        return (linear // n_samp, lax.rem(linear, n_samp))

    def others(act):
        for o in range(1, n_samp):
            act(row, lax.rem(samp + o, n_samp))

    def load(array, which, target):
        return pltpu.make_async_copy(
            array.at[:, pl.ds(pl.multiple_of(target * width, width), width)],
            raw.at[which, target],
            load_sem.at[which, target],
        )

    for which, array in ((0, sketch), (1, probes)):
        for o in range(n_samp):
            load(array, which, lax.rem(samp + 1 + o, n_samp)).start()

    barrier = pltpu.get_barrier_semaphore()

    peers = n_samp - 1
    for o in range(1, n_samp):
        pl.semaphore_signal(
            barrier, inc=1, device_id=(row, lax.rem(samp + o, n_samp)), device_id_type=MESH
        )
    met = [(at(me - 1), (samp == 0) & (row > 0))]
    met += [(at(me + 1), (samp == n_samp - 1) & (row < n_rows - 1))]
    met += [((row + s, samp), (row + s >= 0) & (row + s < n_rows)) for s in shifts]
    for device, valid in met:
        peers = peers + valid.astype(jnp.int32)

        @pl.when(valid)
        def _(device=device):
            pl.semaphore_signal(barrier, inc=1, device_id=device, device_id_type=MESH)

    def exchange(which, send, land, sems):
        def copy(o):
            target = lax.rem(samp + o, n_samp)
            return pltpu.make_async_remote_copy(
                src_ref=send.at[target],
                dst_ref=land.at[samp],
                send_sem=sems.at[0, o],
                recv_sem=sems.at[1, o],
                device_id=(row, target),
                device_id_type=MESH,
            )

        def arrival(o):
            source = lax.rem(samp + n_samp - o, n_samp)
            return pltpu.make_async_remote_copy(
                src_ref=send.at[source],
                dst_ref=land.at[source],
                send_sem=sems.at[0, o],
                recv_sem=sems.at[1, o],
                device_id=(row, source),
                device_id_type=MESH,
            )

        return copy, arrival

    def prepare(array, which, send):
        for o in range(1, n_samp):
            target = lax.rem(samp + o, n_samp)
            load(array, which, target).wait()
            send[target] = raw[which, target].astype(BF16)

    def prepare_own(array, which, hi_ref, lo_ref):
        load(array, which, samp).wait()
        lo_ref[...] = jnp.zeros_like(lo_ref)
        hi, lo = split(raw[which, samp])
        hi_ref[samp] = hi
        lo_ref[samp] = lo

    y_copy, y_arrival = exchange(0, y_send, y_hi, y_sems)
    o_copy, o_arrival = exchange(1, o_send, o_hi, o_sems)

    prepare(sketch, 0, y_send)
    pl.semaphore_wait(barrier, peers)

    for o in range(1, n_samp):
        y_copy(o).start()
    prepare_own(sketch, 0, y_hi, y_lo)
    prepare(probes, 1, o_send)
    prepare_own(probes, 1, o_hi, o_lo)
    for o in range(1, n_samp):
        y_copy(o).wait_send()
    for o in range(1, n_samp):
        o_copy(o).start()
    for o in range(1, n_samp):
        y_arrival(o).wait_recv()

    test_hi, test_lo = split(test_leaf[...])
    both = jnp.concatenate([test_hi, test_lo], axis=0)

    def leaf_columns(ref, i):
        return ref[:, :, i * LEAF : (i + 1) * LEAF].reshape(samples, LEAF)

    blocks, grams = [], []
    for i in range(owned):
        hi, lo = leaf_columns(y_hi, i), leaf_columns(y_lo, i)
        wide = dot_nn(both, hi)
        block = wide[:rank] + (wide[rank:] + dot_nn(test_hi, lo))
        blocks.append(block)
        grams.append(dot_nt(block, block, highest))
    inverses = inverse_factors(grams)
    bases = []
    for i in range(owned):
        basis = dot_nn(inverses[i], blocks[i], highest)
        basis_out[:, i * LEAF : (i + 1) * LEAF] = basis
        hi, lo = split(basis)
        bases.append((hi, jnp.concatenate([hi, lo], axis=0)))

    def project(i, hi_ref, lo_ref):
        hi, pair = bases[i]
        wide = dot_nt(pair, leaf_columns(hi_ref, i))
        return wide[:rank] + (wide[rank:] + dot_nt(hi, leaf_columns(lo_ref, i)))

    for i in range(owned):
        w = project(i, y_hi, y_lo)
        w_buf[i * rank : (i + 1) * rank, :] = w
        put_columns(w_cols, i * rank, w)

    test_coarse = test_parent[...]
    ranges, coarse_grams = [], []
    for p in range(per_device):
        c = dot_nt(test_coarse, w_buf[2 * p * rank : 2 * (p + 1) * rank, :], highest)
        ranges.append(c)
        coarse_grams.append(dot_nt(c, c, highest))

    for o in range(1, n_samp):
        o_copy(o).wait_send()
        o_arrival(o).wait_recv()
    for i in range(owned):
        v = project(i, o_hi, o_lo)
        v_own[i * rank : (i + 1) * rank, :] = v
        v_all[owned + i] = v.astype(BF16)

    def halo(step):
        side = 0 if step == 1 else 1
        return pltpu.make_async_remote_copy(
            src_ref=v_all.at[pl.ds(owned, owned)],
            dst_ref=v_all.at[pl.ds(0 if step == 1 else 2 * owned, owned)],
            send_sem=v_sems.at[0, side],
            recv_sem=v_sems.at[1, side],
            device_id=at(me + step),
            device_id_type=MESH,
        )

    def when(valid, act):
        @pl.when(valid)
        def _():
            act()

    when(me < last, lambda: halo(1).start())
    when(me > 0, lambda: halo(-1).start())

    coarse_inverses = inverse_factors(coarse_grams)
    transfers = []
    for p in range(per_device):
        t = dot_nn(coarse_inverses[p], ranges[p], highest)
        transfer_out[p] = t
        transfers.append(t)
        b = three_pass(dot_nn, t, v_own[2 * p * rank : 2 * (p + 1) * rank, :])
        b_all[REACH, p] = b.astype(BF16)

    def coarse(s):
        return pltpu.make_async_remote_copy(
            src_ref=b_all.at[REACH],
            dst_ref=b_all.at[REACH - s],
            send_sem=b_sems.at[0, REACH - s],
            recv_sem=b_sems.at[1, REACH - s],
            device_id=(row + s, samp),
            device_id_type=MESH,
        )

    def reaches(s):
        return (row + s >= 0) & (row + s < n_rows)

    for s in shifts:
        when(reaches(s), lambda s=s: coarse(s).start())

    for p in range(per_device):
        a = three_pass(dot_nn, transfers[p], w_buf[2 * p * rank : 2 * (p + 1) * rank, :])
        put_columns(a_cols, p * rank, a)

    when(me > 0, lambda: halo(1).wait_recv())
    when(me < last, lambda: halo(-1).wait_recv())
    half = rank // 2
    first_leaf = me * owned
    scale = 1.0 / samples
    for i in range(owned):
        hi, lo = split(even_then_odd(w_cols, i * rank, rank))
        lhs = jnp.concatenate([hi, lo], axis=0)
        for k in range(slots):
            v = v_all[jnp.clip(leaf_far[i, k] - first_leaf + owned, 0, 3 * owned - 1)]
            wide = dot_nt(lhs, v)
            used = jnp.where(k < leaf_count[i], scale, 0.0).astype(F32)
            flatten_rows(flat.at[i], (wide[:rank] + wide[rank:]) * used, k, slots)
        for m in range(half):
            coupling_out[i, :, m * LANES : (m + 1) * LANES] = flat[i, m * slots : (m + 1) * slots, :]

    for s in shifts:
        when(reaches(-s), lambda s=s: coarse(s).wait_recv())
    for p in range(per_device):
        lhs = even_then_odd(a_cols, p * rank, rank).astype(BF16)
        for k in range(slots):
            q = parent_far[p, k]
            from_here = q // (per_device * n_samp) - row + REACH
            b = b_all[jnp.clip(from_here, 0, 2 * REACH), lax.rem(q, per_device)]
            used = jnp.where(k < parent_count[p], scale, 0.0).astype(F32)
            flatten_rows(flat.at[owned + p], dot_nt(lhs, b) * used, k, slots)
        for m in range(half):
            parent_out[p, :, m * LANES : (m + 1) * LANES] = flat[
                owned + p, m * slots : (m + 1) * slots, :
            ]

    when(me < last, lambda: halo(1).wait_send())
    when(me > 0, lambda: halo(-1).wait_send())
    for s in shifts:
        when(reaches(s), lambda s=s: coarse(s).wait_send())


def solution(mesh):
    n_rows, n_samp = mesh.shape["rows"], mesh.shape["samp"]

    def body(sketch, probes, test_leaf, test_parent, leaf_far, leaf_count, parent_far, parent_count):
        rank, samples = test_leaf.shape
        owned, slots = leaf_far.shape
        per_device = parent_far.shape[0]
        local = samples // n_samp
        width = owned * LEAF
        vmem = pl.BlockSpec(memory_space=pltpu.VMEM)
        smem = pl.BlockSpec(memory_space=pltpu.SMEM)
        hbm = pl.BlockSpec(memory_space=pl.ANY)
        blocks = (n_samp, local, width)
        return pl.pallas_call(
            functools.partial(kernel, (n_rows, n_samp)),
            out_shape=(
                jax.ShapeDtypeStruct((rank, width), F32),
                jax.ShapeDtypeStruct((owned, slots, rank * rank), F32),
                jax.ShapeDtypeStruct((per_device, rank, 2 * rank), F32),
                jax.ShapeDtypeStruct((per_device, slots, rank * rank), F32),
            ),
            in_specs=[smem] * 4 + [vmem] * 2 + [hbm] * 2,
            out_specs=(vmem,) * 4,
            scratch_shapes=[
                pltpu.VMEM((2,) + blocks, F32),
                pltpu.VMEM(blocks, BF16),
                pltpu.VMEM(blocks, BF16),
                pltpu.VMEM(blocks, BF16),
                pltpu.VMEM(blocks, BF16),
                pltpu.VMEM(blocks, BF16),
                pltpu.VMEM(blocks, BF16),
                pltpu.VMEM((owned * rank, samples), F32),
                pltpu.VMEM((samples // LANES, owned * rank, LANES), F32),
                pltpu.VMEM((3 * owned, rank, samples), BF16),
                pltpu.VMEM((owned * rank, samples), F32),
                pltpu.VMEM((samples // LANES, per_device * rank, LANES), F32),
                pltpu.VMEM((2 * REACH + 1, per_device, rank, samples), BF16),
                pltpu.VMEM((owned + per_device, slots * rank // 2, LANES), F32),
                pltpu.SemaphoreType.DMA((2, n_samp)),
                pltpu.SemaphoreType.DMA((2, n_samp)),
                pltpu.SemaphoreType.DMA((2, n_samp)),
                pltpu.SemaphoreType.DMA((2, 2)),
                pltpu.SemaphoreType.DMA((2, 2 * REACH + 1)),
            ],
            compiler_params=pltpu.CompilerParams(
                collective_id=0, has_side_effects=True, vmem_limit_bytes=40 * 1024 * 1024
            ),
            cost_estimate=pl.CostEstimate(
                flops=10**9, bytes_accessed=5 * 10**6, transcendentals=0
            ),
        )(leaf_far, leaf_count, parent_far, parent_count, test_leaf, test_parent, sketch, probes)

    return jax.shard_map(
        body,
        mesh=mesh,
        in_specs=(
            P("samp", "rows"),
            P("samp", "rows"),
            P(),
            P(),
            P(("rows", "samp"), None),
            P(("rows", "samp")),
            P(("rows", "samp"), None),
            P(("rows", "samp")),
        ),
        out_specs=(
            P(None, ("rows", "samp")),
            P(("rows", "samp"), None, None),
            P(("rows", "samp"), None, None),
            P(("rows", "samp"), None, None),
        ),
        check_vma=False,
    )
```

```python
import functools

import jax
import jax.numpy as jnp
from jax import lax
from jax.experimental import pallas as pl
from jax.experimental.pallas import tpu as pltpu
from jax.sharding import PartitionSpec as P

LEAF = 256
REACH = 4
LANES = 128

F32 = jnp.float32
BF16 = jnp.bfloat16
MESH = pl.DeviceIdType.MESH
highest = lax.Precision.HIGHEST


def dot_nn(a, b, precision=None):
    return lax.dot_general(
        a, b, (((1,), (0,)), ((), ())), precision=precision, preferred_element_type=F32
    )


def dot_nt(a, b, precision=None):
    return lax.dot_general(
        a, b, (((1,), (1,)), ((), ())), precision=precision, preferred_element_type=F32
    )


def split(x):
    hi = x.astype(BF16)
    return hi, (x - hi.astype(F32)).astype(BF16)


def three_pass(dot, a, b):
    a_hi, a_lo = split(a)
    b_hi, b_lo = split(b)
    return dot(a_hi, b_hi) + (dot(a_lo, b_hi) + dot(a_hi, b_lo))


def row_of(x, s):
    return jnp.broadcast_to(x[s : s + 1, :], x.shape)


def inverse_factors(grams):
    rank = grams[0].shape[0]
    lane = lax.broadcasted_iota(jnp.int32, (8, LANES), 1)
    row = lax.broadcasted_iota(jnp.int32, (8, LANES), 0)
    within = lax.rem(lane, rank)
    base = lane - within
    blocks = rank // 8
    results = []
    pairs = [(grams[i], grams[min(i + 1, len(grams) - 1)]) for i in range(0, len(grams), 2)]
    states = []
    for left, right in pairs:
        whole = jnp.concatenate([left, right], axis=1)
        states.append([whole[8 * t : 8 * t + 8, :] for t in range(blocks)])
    scales = [[None] * blocks for _ in pairs]
    for b in range(blocks):
        in_block = (within >= 8 * b) & (within < 8 * b + 8)
        for at, tiles in enumerate(states):
            tile = tiles[b]
            cols = [
                jnp.take_along_axis(tile, base + (8 * b + j), axis=1, mode="promise_in_bounds")
                for j in range(8)
            ]
            scale = jnp.zeros((8, LANES), F32)
            inv_pivots, heads, pivot_rows = [], [], []
            for s in range(8):
                pivot = row_of(cols[s], s)
                inv_pivot = 1.0 / pivot
                scale = jnp.where(row == s, lax.rsqrt(pivot), scale)
                f = jnp.where(row > s, cols[s] * inv_pivot, 0.0)
                head = [None] * 8
                for j in range(s + 1, 8):
                    head[j] = row_of(cols[j], s)
                    cols[j] = cols[j] - f * head[j]
                here = within == 8 * b + s
                pivot_row = jnp.where(here, 1.0, row_of(tile, s))
                tile = jnp.where(here & (row > s), 0.0, tile) - f * pivot_row
                inv_pivots.append(inv_pivot)
                heads.append(head)
                pivot_rows.append(pivot_row)
            scales[at][b] = scale
            tiles[b] = tile
            for t in range(b + 1, blocks):
                tile = tiles[t]
                cols = [
                    jnp.take_along_axis(tile, base + (8 * b + j), axis=1, mode="promise_in_bounds")
                    for j in range(8)
                ]
                for s in range(8):
                    f = cols[s] * inv_pivots[s]
                    for j in range(s + 1, 8):
                        cols[j] = cols[j] - f * heads[s][j]
                    here = within == 8 * b + s
                    tile = jnp.where(here, 0.0, tile) - f * pivot_rows[s]
                tiles[t] = tile
    for at, tiles in enumerate(states):
        done = []
        for b in range(blocks):
            lower = jnp.where(within < row + 8 * b, tiles[b], 0.0)
            lower = jnp.where(within == row + 8 * b, 1.0, lower)
            done.append(lower * scales[at][b])
        whole = jnp.concatenate(done, axis=0)
        results += [whole[:, :rank], whole[:, rank : 2 * rank]]
    return results[: len(grams)]


def put_columns(ref, first, value):
    for c in range(value.shape[1] // LANES):
        ref[c, first : first + value.shape[0], :] = value[:, c * LANES : (c + 1) * LANES]


def even_then_odd(ref, first, rows):
    parts = [
        jnp.concatenate(
            [ref[c, pl.ds(first + o, rows // 2, stride=2), :] for o in (0, 1)], axis=0
        )
        for c in range(ref.shape[0])
    ]
    return jnp.concatenate(parts, axis=1)


def flatten_rows(ref, product, slot, slots):
    half = product.shape[0] // 2
    packed = jnp.concatenate([product[:half], product[half:]], axis=1)
    ref[pl.ds(slot, half, stride=slots), :] = packed


def kernel(
    sizes,
    far_in, count_in, coarse_far_in, coarse_count_in, test_in, test_coarse_in, sketch, probes,
    basis_out, coupling_out, transfer_out, parent_out,
    raw, y_send, o_send, y_hi, y_lo, o_hi, o_lo, w_buf, w_cols, v_all, v_own, a_cols, b_all, flat,
    leaf_far, leaf_count, parent_far, parent_count, test_leaf, test_parent,
    load_sem, small_sem, y_sems, o_sems, v_sems, b_sems,
):
    n_rows, n_samp = sizes
    owned, slots = leaf_far.shape
    per_device = parent_far.shape[0]
    rank, samples = test_leaf.shape
    local = samples // n_samp
    width = owned * LEAF
    row, samp = lax.axis_index("rows"), lax.axis_index("samp")
    me = row * n_samp + samp
    last = n_rows * n_samp - 1
    shifts = [s for s in range(-REACH, REACH + 1) if s != 0]

    def at(linear):
        return (linear // n_samp, lax.rem(linear, n_samp))

    def others(act):
        for o in range(1, n_samp):
            act(row, lax.rem(samp + o, n_samp))

    def load(array, which, target):
        return pltpu.make_async_copy(
            array.at[:, pl.ds(pl.multiple_of(target * width, width), width)],
            raw.at[which, target],
            load_sem.at[which, target],
        )

    for which, array in ((0, sketch), (1, probes)):
        for o in range(n_samp):
            load(array, which, lax.rem(samp + 1 + o, n_samp)).start()

    small = [
        pltpu.make_async_copy(source, target, small_sem.at[i])
        for i, (source, target) in enumerate((
            (test_in, test_leaf),
            (test_coarse_in, test_parent),
            (far_in, leaf_far),
            (count_in, leaf_count),
            (coarse_far_in, parent_far),
            (coarse_count_in, parent_count),
        ))
    ]
    for copy in small:
        copy.start()

    barrier = pltpu.get_barrier_semaphore()

    peers = n_samp - 1
    for o in range(1, n_samp):
        pl.semaphore_signal(
            barrier, inc=1, device_id=(row, lax.rem(samp + o, n_samp)), device_id_type=MESH
        )
    met = [(at(me - 1), (samp == 0) & (row > 0))]
    met += [(at(me + 1), (samp == n_samp - 1) & (row < n_rows - 1))]
    met += [((row + s, samp), (row + s >= 0) & (row + s < n_rows)) for s in shifts]
    for device, valid in met:
        peers = peers + valid.astype(jnp.int32)

        @pl.when(valid)
        def _(device=device):
            pl.semaphore_signal(barrier, inc=1, device_id=device, device_id_type=MESH)

    def exchange(which, send, land, sems):
        def copy(o):
            target = lax.rem(samp + o, n_samp)
            return pltpu.make_async_remote_copy(
                src_ref=send.at[target],
                dst_ref=land.at[samp],
                send_sem=sems.at[0, o],
                recv_sem=sems.at[1, o],
                device_id=(row, target),
                device_id_type=MESH,
            )

        def arrival(o):
            source = lax.rem(samp + n_samp - o, n_samp)
            return pltpu.make_async_remote_copy(
                src_ref=send.at[source],
                dst_ref=land.at[source],
                send_sem=sems.at[0, o],
                recv_sem=sems.at[1, o],
                device_id=(row, source),
                device_id_type=MESH,
            )

        return copy, arrival

    def prepare(array, which, send):
        for o in range(1, n_samp):
            target = lax.rem(samp + o, n_samp)
            load(array, which, target).wait()
            send[target] = raw[which, target].astype(BF16)

    def prepare_own(array, which, hi_ref, lo_ref):
        load(array, which, samp).wait()
        lo_ref[...] = jnp.zeros_like(lo_ref)
        hi, lo = split(raw[which, samp])
        hi_ref[samp] = hi
        lo_ref[samp] = lo

    y_copy, y_arrival = exchange(0, y_send, y_hi, y_sems)
    o_copy, o_arrival = exchange(1, o_send, o_hi, o_sems)

    prepare(sketch, 0, y_send)
    pl.semaphore_wait(barrier, peers)

    for o in range(1, n_samp):
        y_copy(o).start()
    prepare_own(sketch, 0, y_hi, y_lo)
    prepare(probes, 1, o_send)
    prepare_own(probes, 1, o_hi, o_lo)
    for o in range(1, n_samp):
        y_copy(o).wait_send()
    for o in range(1, n_samp):
        o_copy(o).start()
    for o in range(1, n_samp):
        y_arrival(o).wait_recv()

    for copy in small:
        copy.wait()

    test_hi, test_lo = split(test_leaf[...])
    both = jnp.concatenate([test_hi, test_lo], axis=0)

    def leaf_columns(ref, i):
        return ref[:, :, i * LEAF : (i + 1) * LEAF].reshape(samples, LEAF)

    blocks, grams = [], []
    for i in range(owned):
        hi, lo = leaf_columns(y_hi, i), leaf_columns(y_lo, i)
        wide = dot_nn(both, hi)
        block = wide[:rank] + (wide[rank:] + dot_nn(test_hi, lo))
        blocks.append(block)
        grams.append(dot_nt(block, block, highest))
    inverses = inverse_factors(grams)
    bases = []
    for i in range(owned):
        basis = dot_nn(inverses[i], blocks[i], highest)
        basis_out[:, i * LEAF : (i + 1) * LEAF] = basis
        hi, lo = split(basis)
        bases.append((hi, jnp.concatenate([hi, lo], axis=0)))

    def project(i, hi_ref, lo_ref):
        hi, pair = bases[i]
        wide = dot_nt(pair, leaf_columns(hi_ref, i))
        return wide[:rank] + (wide[rank:] + dot_nt(hi, leaf_columns(lo_ref, i)))

    for i in range(owned):
        w = project(i, y_hi, y_lo)
        w_buf[i * rank : (i + 1) * rank, :] = w
        put_columns(w_cols, i * rank, w)

    test_coarse = test_parent[...]
    ranges, coarse_grams = [], []
    for p in range(per_device):
        c = dot_nt(test_coarse, w_buf[2 * p * rank : 2 * (p + 1) * rank, :], highest)
        ranges.append(c)
        coarse_grams.append(dot_nt(c, c, highest))

    for o in range(1, n_samp):
        o_copy(o).wait_send()
        o_arrival(o).wait_recv()
    for i in range(owned):
        v = project(i, o_hi, o_lo)
        v_own[i * rank : (i + 1) * rank, :] = v
        v_all[owned + i] = v.astype(BF16)

    def halo(step):
        side = 0 if step == 1 else 1
        return pltpu.make_async_remote_copy(
            src_ref=v_all.at[pl.ds(owned, owned)],
            dst_ref=v_all.at[pl.ds(0 if step == 1 else 2 * owned, owned)],
            send_sem=v_sems.at[0, side],
            recv_sem=v_sems.at[1, side],
            device_id=at(me + step),
            device_id_type=MESH,
        )

    def when(valid, act):
        @pl.when(valid)
        def _():
            act()

    when(me < last, lambda: halo(1).start())
    when(me > 0, lambda: halo(-1).start())

    coarse_inverses = inverse_factors(coarse_grams)
    transfers = []
    for p in range(per_device):
        t = dot_nn(coarse_inverses[p], ranges[p], highest)
        transfer_out[p] = t
        transfers.append(t)
        b = three_pass(dot_nn, t, v_own[2 * p * rank : 2 * (p + 1) * rank, :])
        b_all[REACH, p] = b.astype(BF16)

    def coarse(s):
        return pltpu.make_async_remote_copy(
            src_ref=b_all.at[REACH],
            dst_ref=b_all.at[REACH - s],
            send_sem=b_sems.at[0, REACH - s],
            recv_sem=b_sems.at[1, REACH - s],
            device_id=(row + s, samp),
            device_id_type=MESH,
        )

    def reaches(s):
        return (row + s >= 0) & (row + s < n_rows)

    for s in shifts:
        when(reaches(s), lambda s=s: coarse(s).start())

    for p in range(per_device):
        a = three_pass(dot_nn, transfers[p], w_buf[2 * p * rank : 2 * (p + 1) * rank, :])
        put_columns(a_cols, p * rank, a)

    when(me > 0, lambda: halo(1).wait_recv())
    when(me < last, lambda: halo(-1).wait_recv())
    half = rank // 2
    first_leaf = me * owned
    scale = 1.0 / samples
    for i in range(owned):
        hi, lo = split(even_then_odd(w_cols, i * rank, rank))
        lhs = jnp.concatenate([hi, lo], axis=0)
        for k in range(slots):
            v = v_all[jnp.clip(leaf_far[i, k] - first_leaf + owned, 0, 3 * owned - 1)]
            wide = dot_nt(lhs, v)
            used = jnp.where(k < leaf_count[i], scale, 0.0).astype(F32)
            flatten_rows(flat.at[i], (wide[:rank] + wide[rank:]) * used, k, slots)
        for m in range(half):
            coupling_out[i, :, m * LANES : (m + 1) * LANES] = flat[i, m * slots : (m + 1) * slots, :]

    for s in shifts:
        when(reaches(-s), lambda s=s: coarse(s).wait_recv())
    for p in range(per_device):
        hi, lo = split(even_then_odd(a_cols, p * rank, rank))
        lhs = jnp.concatenate([hi, lo], axis=0)
        for k in range(slots):
            q = parent_far[p, k]
            from_here = q // (per_device * n_samp) - row + REACH
            b = b_all[jnp.clip(from_here, 0, 2 * REACH), lax.rem(q, per_device)]
            used = jnp.where(k < parent_count[p], scale, 0.0).astype(F32)
            wide = dot_nt(lhs, b)
            flatten_rows(flat.at[owned + p], (wide[:rank] + wide[rank:]) * used, k, slots)
        for m in range(half):
            parent_out[p, :, m * LANES : (m + 1) * LANES] = flat[
                owned + p, m * slots : (m + 1) * slots, :
            ]

    when(me < last, lambda: halo(1).wait_send())
    when(me > 0, lambda: halo(-1).wait_send())
    for s in shifts:
        when(reaches(s), lambda s=s: coarse(s).wait_send())


def hand_over(*refs):
    copies = [pltpu.make_async_copy(refs[i], refs[4 + i], refs[8].at[i]) for i in range(4)]
    for copy in copies:
        copy.start()
    for copy in copies:
        copy.wait()


def solution(mesh):
    n_rows, n_samp = mesh.shape["rows"], mesh.shape["samp"]

    def body(sketch, probes, test_leaf, test_parent, leaf_far, leaf_count, parent_far, parent_count):
        rank, samples = test_leaf.shape
        owned, slots = leaf_far.shape
        per_device = parent_far.shape[0]
        local = samples // n_samp
        width = owned * LEAF
        vmem = pl.BlockSpec(memory_space=pltpu.VMEM)
        hbm = pl.BlockSpec(memory_space=pltpu.HBM)
        blocks = (n_samp, local, width)
        made = pl.pallas_call(
            functools.partial(kernel, (n_rows, n_samp)),
            out_shape=(
                jax.ShapeDtypeStruct((rank, width), F32),
                jax.ShapeDtypeStruct((owned, slots, rank * rank), F32),
                jax.ShapeDtypeStruct((per_device, rank, 2 * rank), F32),
                jax.ShapeDtypeStruct((per_device, slots, rank * rank), F32),
            ),
            in_specs=[hbm] * 8,
            out_specs=(vmem,) * 4,
            scratch_shapes=[
                pltpu.VMEM((2,) + blocks, F32),
                pltpu.VMEM(blocks, BF16),
                pltpu.VMEM(blocks, BF16),
                pltpu.VMEM(blocks, BF16),
                pltpu.VMEM(blocks, BF16),
                pltpu.VMEM(blocks, BF16),
                pltpu.VMEM(blocks, BF16),
                pltpu.VMEM((owned * rank, samples), F32),
                pltpu.VMEM((samples // LANES, owned * rank, LANES), F32),
                pltpu.VMEM((3 * owned, rank, samples), BF16),
                pltpu.VMEM((owned * rank, samples), F32),
                pltpu.VMEM((samples // LANES, per_device * rank, LANES), F32),
                pltpu.VMEM((2 * REACH + 1, per_device, rank, samples), BF16),
                pltpu.VMEM((owned + per_device, slots * rank // 2, LANES), F32),
                pltpu.SMEM(leaf_far.shape, jnp.int32),
                pltpu.SMEM(leaf_count.shape, jnp.int32),
                pltpu.SMEM(parent_far.shape, jnp.int32),
                pltpu.SMEM(parent_count.shape, jnp.int32),
                pltpu.VMEM(test_leaf.shape, F32),
                pltpu.VMEM(test_parent.shape, F32),
                pltpu.SemaphoreType.DMA((2, n_samp)),
                pltpu.SemaphoreType.DMA((6,)),
                pltpu.SemaphoreType.DMA((2, n_samp)),
                pltpu.SemaphoreType.DMA((2, n_samp)),
                pltpu.SemaphoreType.DMA((2, 2)),
                pltpu.SemaphoreType.DMA((2, 2 * REACH + 1)),
            ],
            compiler_params=pltpu.CompilerParams(
                collective_id=0, has_side_effects=True, vmem_limit_bytes=62 * 1024 * 1024
            ),
            cost_estimate=pl.CostEstimate(
                flops=10**9, bytes_accessed=5 * 10**6, transcendentals=0
            ),
        )(leaf_far, leaf_count, parent_far, parent_count, test_leaf, test_parent, sketch, probes)
        return pl.pallas_call(
            hand_over,
            out_shape=tuple(jax.ShapeDtypeStruct(x.shape, x.dtype) for x in made),
            in_specs=[hbm] * 4,
            out_specs=(hbm,) * 4,
            scratch_shapes=[pltpu.SemaphoreType.DMA((4,))],
            compiler_params=pltpu.CompilerParams(vmem_limit_bytes=62 * 1024 * 1024),
        )(*made)

    return jax.shard_map(
        body,
        mesh=mesh,
        in_specs=(
            P("samp", "rows"),
            P("samp", "rows"),
            P(),
            P(),
            P(("rows", "samp"), None),
            P(("rows", "samp")),
            P(("rows", "samp"), None),
            P(("rows", "samp")),
        ),
        out_specs=(
            P(None, ("rows", "samp")),
            P(("rows", "samp"), None, None),
            P(("rows", "samp"), None, None),
            P(("rows", "samp"), None, None),
        ),
        check_vma=False,
    )
```

```python
import functools

import jax
import jax.numpy as jnp
from jax import lax
from jax.experimental import pallas as pl
from jax.experimental.pallas import tpu as pltpu
from jax.sharding import PartitionSpec as P

LEAF = 256
REACH = 4
LANES = 128

F32 = jnp.float32
BF16 = jnp.bfloat16
MESH = pl.DeviceIdType.MESH
highest = lax.Precision.HIGHEST


def dot_nn(a, b, precision=None):
    return lax.dot_general(
        a, b, (((1,), (0,)), ((), ())), precision=precision, preferred_element_type=F32
    )


def dot_nt(a, b, precision=None):
    return lax.dot_general(
        a, b, (((1,), (1,)), ((), ())), precision=precision, preferred_element_type=F32
    )


def split(x):
    hi = x.astype(BF16)
    return hi, (x - hi.astype(F32)).astype(BF16)


def three_pass(dot, a, b):
    a_hi, a_lo = split(a)
    b_hi, b_lo = split(b)
    return dot(a_hi, b_hi) + (dot(a_lo, b_hi) + dot(a_hi, b_lo))


def row_of(x, s):
    return jnp.broadcast_to(x[s : s + 1, :], x.shape)


def inverse_factors(grams):
    rank = grams[0].shape[0]
    lane = lax.broadcasted_iota(jnp.int32, (8, LANES), 1)
    row = lax.broadcasted_iota(jnp.int32, (8, LANES), 0)
    within = lax.rem(lane, rank)
    base = lane - within
    blocks = rank // 8
    results = []
    pairs = [(grams[i], grams[min(i + 1, len(grams) - 1)]) for i in range(0, len(grams), 2)]
    states = []
    for left, right in pairs:
        whole = jnp.concatenate([left, right], axis=1)
        states.append([whole[8 * t : 8 * t + 8, :] for t in range(blocks)])
    scales = [[None] * blocks for _ in pairs]
    for b in range(blocks):
        in_block = (within >= 8 * b) & (within < 8 * b + 8)
        for at, tiles in enumerate(states):
            tile = tiles[b]
            cols = [
                jnp.take_along_axis(tile, base + (8 * b + j), axis=1, mode="promise_in_bounds")
                for j in range(8)
            ]
            scale = jnp.zeros((8, LANES), F32)
            inv_pivots, heads, pivot_rows = [], [], []
            for s in range(8):
                pivot = row_of(cols[s], s)
                inv_pivot = 1.0 / pivot
                scale = jnp.where(row == s, lax.rsqrt(pivot), scale)
                f = jnp.where(row > s, cols[s] * inv_pivot, 0.0)
                head = [None] * 8
                for j in range(s + 1, 8):
                    head[j] = row_of(cols[j], s)
                    cols[j] = cols[j] - f * head[j]
                here = within == 8 * b + s
                pivot_row = jnp.where(here, 1.0, row_of(tile, s))
                tile = jnp.where(here & (row > s), 0.0, tile) - f * pivot_row
                inv_pivots.append(inv_pivot)
                heads.append(head)
                pivot_rows.append(pivot_row)
            scales[at][b] = scale
            tiles[b] = tile
            for t in range(b + 1, blocks):
                tile = tiles[t]
                cols = [
                    jnp.take_along_axis(tile, base + (8 * b + j), axis=1, mode="promise_in_bounds")
                    for j in range(8)
                ]
                for s in range(8):
                    f = cols[s] * inv_pivots[s]
                    for j in range(s + 1, 8):
                        cols[j] = cols[j] - f * heads[s][j]
                    here = within == 8 * b + s
                    tile = jnp.where(here, 0.0, tile) - f * pivot_rows[s]
                tiles[t] = tile
    for at, tiles in enumerate(states):
        done = []
        for b in range(blocks):
            lower = jnp.where(within < row + 8 * b, tiles[b], 0.0)
            lower = jnp.where(within == row + 8 * b, 1.0, lower)
            done.append(lower * scales[at][b])
        whole = jnp.concatenate(done, axis=0)
        results += [whole[:, :rank], whole[:, rank : 2 * rank]]
    return results[: len(grams)]


def put_columns(ref, first, value):
    for c in range(value.shape[1] // LANES):
        ref[c, first : first + value.shape[0], :] = value[:, c * LANES : (c + 1) * LANES]


def even_then_odd(ref, first, rows):
    parts = [
        jnp.concatenate(
            [ref[c, pl.ds(first + o, rows // 2, stride=2), :] for o in (0, 1)], axis=0
        )
        for c in range(ref.shape[0])
    ]
    return jnp.concatenate(parts, axis=1)


def flatten_rows(ref, product, slot, slots):
    half = product.shape[0] // 2
    packed = jnp.concatenate([product[:half], product[half:]], axis=1)
    ref[pl.ds(slot, half, stride=slots), :] = packed


def kernel(
    sizes,
    far_in, count_in, coarse_far_in, coarse_count_in, test_in, test_coarse_in, sketch, probes,
    basis_out, coupling_out, transfer_out, parent_out,
    raw, y_send, o_send, y_hi, y_lo, o_hi, o_lo, w_buf, w_cols, v_all, v_own, a_cols, b_all, flat,
    leaf_far, leaf_count, parent_far, parent_count, test_leaf, test_parent,
    load_sem, small_sem, y_sems, o_sems, v_sems, b_sems,
):
    n_rows, n_samp = sizes
    owned, slots = leaf_far.shape
    per_device = parent_far.shape[0]
    rank, samples = test_leaf.shape
    local = samples // n_samp
    width = owned * LEAF
    row, samp = lax.axis_index("rows"), lax.axis_index("samp")
    me = row * n_samp + samp
    last = n_rows * n_samp - 1
    shifts = [s for s in range(-REACH, REACH + 1) if s != 0]

    def at(linear):
        return (linear // n_samp, lax.rem(linear, n_samp))

    def others(act):
        for o in range(1, n_samp):
            act(row, lax.rem(samp + o, n_samp))

    def load(array, which, target):
        return pltpu.make_async_copy(
            array.at[:, pl.ds(pl.multiple_of(target * width, width), width)],
            raw.at[which, target],
            load_sem.at[which, target],
        )

    for which, array in ((0, sketch), (1, probes)):
        for o in range(n_samp):
            load(array, which, lax.rem(samp + 1 + o, n_samp)).start()

    small = [
        pltpu.make_async_copy(source, target, small_sem.at[i])
        for i, (source, target) in enumerate((
            (test_in, test_leaf),
            (test_coarse_in, test_parent),
            (far_in, leaf_far),
            (count_in, leaf_count),
            (coarse_far_in, parent_far),
            (coarse_count_in, parent_count),
        ))
    ]
    for copy in small:
        copy.start()

    barrier = pltpu.get_barrier_semaphore()

    peers = n_samp - 1
    for o in range(1, n_samp):
        pl.semaphore_signal(
            barrier, inc=1, device_id=(row, lax.rem(samp + o, n_samp)), device_id_type=MESH
        )
    met = [(at(me - 1), (samp == 0) & (row > 0))]
    met += [(at(me + 1), (samp == n_samp - 1) & (row < n_rows - 1))]
    met += [((row + s, samp), (row + s >= 0) & (row + s < n_rows)) for s in shifts]
    for device, valid in met:
        peers = peers + valid.astype(jnp.int32)

        @pl.when(valid)
        def _(device=device):
            pl.semaphore_signal(barrier, inc=1, device_id=device, device_id_type=MESH)

    def exchange(which, send, land, sems):
        def copy(o):
            target = lax.rem(samp + o, n_samp)
            return pltpu.make_async_remote_copy(
                src_ref=send.at[target],
                dst_ref=land.at[samp],
                send_sem=sems.at[0, o],
                recv_sem=sems.at[1, o],
                device_id=(row, target),
                device_id_type=MESH,
            )

        def arrival(o):
            source = lax.rem(samp + n_samp - o, n_samp)
            return pltpu.make_async_remote_copy(
                src_ref=send.at[source],
                dst_ref=land.at[source],
                send_sem=sems.at[0, o],
                recv_sem=sems.at[1, o],
                device_id=(row, source),
                device_id_type=MESH,
            )

        return copy, arrival

    def prepare(array, which, send):
        for o in range(1, n_samp):
            target = lax.rem(samp + o, n_samp)
            load(array, which, target).wait()
            send[target] = raw[which, target].astype(BF16)

    def prepare_own(array, which, hi_ref, lo_ref):
        load(array, which, samp).wait()
        lo_ref[...] = jnp.zeros_like(lo_ref)
        hi, lo = split(raw[which, samp])
        hi_ref[samp] = hi
        lo_ref[samp] = lo

    y_copy, y_arrival = exchange(0, y_send, y_hi, y_sems)
    o_copy, o_arrival = exchange(1, o_send, o_hi, o_sems)

    prepare(sketch, 0, y_send)
    pl.semaphore_wait(barrier, peers)

    for o in range(1, n_samp):
        y_copy(o).start()
    prepare_own(sketch, 0, y_hi, y_lo)
    prepare(probes, 1, o_send)
    prepare_own(probes, 1, o_hi, o_lo)
    for o in range(1, n_samp):
        y_copy(o).wait_send()
    for o in range(1, n_samp):
        o_copy(o).start()
    for o in range(1, n_samp):
        y_arrival(o).wait_recv()

    for copy in small:
        copy.wait()

    test_hi, test_lo = split(test_leaf[...])
    both = jnp.concatenate([test_hi, test_lo], axis=0)

    def leaf_columns(ref, i):
        return ref[:, :, i * LEAF : (i + 1) * LEAF].reshape(samples, LEAF)

    blocks, grams = [], []
    for i in range(owned):
        hi, lo = leaf_columns(y_hi, i), leaf_columns(y_lo, i)
        wide = dot_nn(both, hi)
        block = wide[:rank] + (wide[rank:] + dot_nn(test_hi, lo))
        blocks.append(block)
        grams.append(dot_nt(block, block, highest))
    inverses = inverse_factors(grams)
    bases = []
    for i in range(owned):
        basis = dot_nn(inverses[i], blocks[i], highest)
        basis_out[:, i * LEAF : (i + 1) * LEAF] = basis
        hi, lo = split(basis)
        bases.append((hi, jnp.concatenate([hi, lo], axis=0)))

    def project(i, hi_ref, lo_ref):
        hi, pair = bases[i]
        wide = dot_nt(pair, leaf_columns(hi_ref, i))
        return wide[:rank] + (wide[rank:] + dot_nt(hi, leaf_columns(lo_ref, i)))

    for i in range(owned):
        w = project(i, y_hi, y_lo)
        w_buf[i * rank : (i + 1) * rank, :] = w
        put_columns(w_cols, i * rank, w)

    test_coarse = test_parent[...]
    ranges, coarse_grams = [], []
    for p in range(per_device):
        c = dot_nt(test_coarse, w_buf[2 * p * rank : 2 * (p + 1) * rank, :], highest)
        ranges.append(c)
        coarse_grams.append(dot_nt(c, c, highest))

    for o in range(1, n_samp):
        o_copy(o).wait_send()
        o_arrival(o).wait_recv()
    for i in range(owned):
        v = project(i, o_hi, o_lo)
        v_own[i * rank : (i + 1) * rank, :] = v
        v_all[owned + i] = v.astype(BF16)

    def halo(step):
        side = 0 if step == 1 else 1
        return pltpu.make_async_remote_copy(
            src_ref=v_all.at[pl.ds(owned, owned)],
            dst_ref=v_all.at[pl.ds(0 if step == 1 else 2 * owned, owned)],
            send_sem=v_sems.at[0, side],
            recv_sem=v_sems.at[1, side],
            device_id=at(me + step),
            device_id_type=MESH,
        )

    def when(valid, act):
        @pl.when(valid)
        def _():
            act()

    when(me < last, lambda: halo(1).start())
    when(me > 0, lambda: halo(-1).start())

    coarse_inverses = inverse_factors(coarse_grams)
    transfers = []
    for p in range(per_device):
        t = dot_nn(coarse_inverses[p], ranges[p], highest)
        transfer_out[p] = t
        transfers.append(t)
        b = three_pass(dot_nn, t, v_own[2 * p * rank : 2 * (p + 1) * rank, :])
        b_all[REACH, p] = b.astype(BF16)

    def coarse(s):
        return pltpu.make_async_remote_copy(
            src_ref=b_all.at[REACH],
            dst_ref=b_all.at[REACH - s],
            send_sem=b_sems.at[0, REACH - s],
            recv_sem=b_sems.at[1, REACH - s],
            device_id=(row + s, samp),
            device_id_type=MESH,
        )

    def reaches(s):
        return (row + s >= 0) & (row + s < n_rows)

    for s in shifts:
        when(reaches(s), lambda s=s: coarse(s).start())

    for p in range(per_device):
        a = three_pass(dot_nn, transfers[p], w_buf[2 * p * rank : 2 * (p + 1) * rank, :])
        put_columns(a_cols, p * rank, a)

    when(me > 0, lambda: halo(1).wait_recv())
    when(me < last, lambda: halo(-1).wait_recv())
    half = rank // 2
    first_leaf = me * owned
    scale = 1.0 / samples
    for i in range(owned):
        hi, lo = split(even_then_odd(w_cols, i * rank, rank))
        lhs = jnp.concatenate([hi, lo], axis=0)
        for k in range(slots):
            v = v_all[jnp.clip(leaf_far[i, k] - first_leaf + owned, 0, 3 * owned - 1)]
            wide = dot_nt(lhs, v)
            used = jnp.where(k < leaf_count[i], scale, 0.0).astype(F32)
            flatten_rows(flat.at[i], (wide[:rank] + wide[rank:]) * used, k, slots)
        for m in range(half):
            coupling_out[i, :, m * LANES : (m + 1) * LANES] = flat[i, m * slots : (m + 1) * slots, :]

    for s in shifts:
        when(reaches(-s), lambda s=s: coarse(s).wait_recv())
    for p in range(per_device):
        hi, lo = split(even_then_odd(a_cols, p * rank, rank))
        lhs = jnp.concatenate([hi, lo], axis=0)
        for k in range(slots):
            q = parent_far[p, k]
            from_here = q // (per_device * n_samp) - row + REACH
            b = b_all[jnp.clip(from_here, 0, 2 * REACH), lax.rem(q, per_device)]
            used = jnp.where(k < parent_count[p], scale, 0.0).astype(F32)
            wide = dot_nt(lhs, b)
            flatten_rows(flat.at[owned + p], (wide[:rank] + wide[rank:]) * used, k, slots)
        for m in range(half):
            parent_out[p, :, m * LANES : (m + 1) * LANES] = flat[
                owned + p, m * slots : (m + 1) * slots, :
            ]

    when(me < last, lambda: halo(1).wait_send())
    when(me > 0, lambda: halo(-1).wait_send())
    for s in shifts:
        when(reaches(s), lambda s=s: coarse(s).wait_send())


def solution(mesh):
    n_rows, n_samp = mesh.shape["rows"], mesh.shape["samp"]

    def body(sketch, probes, test_leaf, test_parent, leaf_far, leaf_count, parent_far, parent_count):
        rank, samples = test_leaf.shape
        owned, slots = leaf_far.shape
        per_device = parent_far.shape[0]
        local = samples // n_samp
        width = owned * LEAF
        vmem = pl.BlockSpec(memory_space=pltpu.VMEM)
        hbm = pl.BlockSpec(memory_space=pltpu.HBM)
        blocks = (n_samp, local, width)
        return pl.pallas_call(
            functools.partial(kernel, (n_rows, n_samp)),
            out_shape=(
                jax.ShapeDtypeStruct((rank, width), F32),
                jax.ShapeDtypeStruct((owned, slots, rank * rank), F32),
                jax.ShapeDtypeStruct((per_device, rank, 2 * rank), F32),
                jax.ShapeDtypeStruct((per_device, slots, rank * rank), F32),
            ),
            in_specs=[hbm] * 8,
            out_specs=(vmem,) * 4,
            scratch_shapes=[
                pltpu.VMEM((2,) + blocks, F32),
                pltpu.VMEM(blocks, BF16),
                pltpu.VMEM(blocks, BF16),
                pltpu.VMEM(blocks, BF16),
                pltpu.VMEM(blocks, BF16),
                pltpu.VMEM(blocks, BF16),
                pltpu.VMEM(blocks, BF16),
                pltpu.VMEM((owned * rank, samples), F32),
                pltpu.VMEM((samples // LANES, owned * rank, LANES), F32),
                pltpu.VMEM((3 * owned, rank, samples), BF16),
                pltpu.VMEM((owned * rank, samples), F32),
                pltpu.VMEM((samples // LANES, per_device * rank, LANES), F32),
                pltpu.VMEM((2 * REACH + 1, per_device, rank, samples), BF16),
                pltpu.VMEM((owned + per_device, slots * rank // 2, LANES), F32),
                pltpu.SMEM(leaf_far.shape, jnp.int32),
                pltpu.SMEM(leaf_count.shape, jnp.int32),
                pltpu.SMEM(parent_far.shape, jnp.int32),
                pltpu.SMEM(parent_count.shape, jnp.int32),
                pltpu.VMEM(test_leaf.shape, F32),
                pltpu.VMEM(test_parent.shape, F32),
                pltpu.SemaphoreType.DMA((2, n_samp)),
                pltpu.SemaphoreType.DMA((6,)),
                pltpu.SemaphoreType.DMA((2, n_samp)),
                pltpu.SemaphoreType.DMA((2, n_samp)),
                pltpu.SemaphoreType.DMA((2, 2)),
                pltpu.SemaphoreType.DMA((2, 2 * REACH + 1)),
            ],
            compiler_params=pltpu.CompilerParams(
                collective_id=0, has_side_effects=True, vmem_limit_bytes=62 * 1024 * 1024
            ),
            cost_estimate=pl.CostEstimate(
                flops=10**9, bytes_accessed=5 * 10**6, transcendentals=0
            ),
        )(leaf_far, leaf_count, parent_far, parent_count, test_leaf, test_parent, sketch, probes)

    return jax.shard_map(
        body,
        mesh=mesh,
        in_specs=(
            P("samp", "rows"),
            P("samp", "rows"),
            P(),
            P(),
            P(("rows", "samp"), None),
            P(("rows", "samp")),
            P(("rows", "samp"), None),
            P(("rows", "samp")),
        ),
        out_specs=(
            P(None, ("rows", "samp")),
            P(("rows", "samp"), None, None),
            P(("rows", "samp"), None, None),
            P(("rows", "samp"), None, None),
        ),
        check_vma=False,
    )
```
